256 devices in a mesh: pipe: 32 (over x, y, core), uly: 8 (over z).
Axes of the slice: x: 4, y: 4, z: 8, core: 2. Of those that a mesh axis runs over, the one named last changes fastest.
Arguments:
- fresh_qkv: bfloat16 [8192, 3, 3072], P(('pipe', 'uly')), may hold values from -8 to 8
- stale_cache: bfloat16 [32, 8192, 2, 3072], P('pipe', None, None, 'uly'), may hold values from -8 to 8
- plan: int32 [32], replicated, may hold values from 0 to 31, as said below
- refresh: int32 [32, 6], P('pipe'), may hold values from -1 to 31, as said below
Outputs:
- attended: bfloat16 [8192, 3072], P(('pipe', 'uly'))
The draws below stay inside these ranges and needn't reach their ends.
Inputs may be any that keep to these rules, and one draw needn't show every extreme that they name: `plan`: a permutation of the patch ids. `refresh`: each row lists distinct ids, never the section's own patch, only patches held by sections at distance 1 to 3 along the sections, cyclically; rows hold from 0 to 6 ids, and some row holds 6.
All inputs are finite; a program needn't handle non-finite values.
Results may differ from the reference program's by a relative error of at most 0.0029.
Values may be sent and summed in bfloat16 or wider, within the bound.
No kernel may reach another device: no remote copies, remote signals or barrier semaphores. Data moves between devices by JAX's collectives and lax.ppermute only.
A program may use at most 128 MiB of HBM per device.

```python
import math
import jax
import jax.numpy as jnp
from jax import lax

HEADS = 24
HD = 128
PT = 256
SPAN = 3
WIDTH = 3072
SLOTS = 6
TOTAL = 8192
N_PIPE = 32


def patch_order(key):
    return jax.random.permutation(key, N_PIPE).astype(jnp.int32)


def draw_plan(key, part):
    return patch_order(key)


def draw_refresh(key, part):
    order = patch_order(key)
    key = jax.random.fold_in(key, 7)
    first_key, second_key, third_key = jax.random.split(key, 3)
    steps_up = jnp.arange(1, SPAN + 1, dtype=jnp.int32)
    offsets = jnp.concatenate([steps_up, -steps_up])
    sections = jnp.arange(N_PIPE, dtype=jnp.int32)
    holders = (sections[:, None] - offsets[None, :]) % N_PIPE
    ids = order[holders]
    keep = jax.random.randint(first_key, (N_PIPE, SLOTS), 0, 2) == 1
    full_row = jax.random.randint(second_key, (), 0, N_PIPE)
    keep = keep | (sections[:, None] == full_row)
    ids = jnp.where(keep, ids, -1)
    ranks = jax.random.randint(third_key, (N_PIPE, SLOTS), 0, 1048576) * SLOTS + jnp.arange(SLOTS, dtype=jnp.int32)[None, :]
    shuffle = jnp.argsort(ranks, axis=1)
    return jnp.take_along_axis(ids, shuffle, axis=1).astype(jnp.int32)


def draw_fresh_qkv(key, part):
    key = jax.random.fold_in(key, 11)
    base_key = jax.random.fold_in(key, 0)
    whole = jnp.clip(1.75 * jax.random.normal(base_key, (TOTAL, 3, WIDTH), jnp.float32), -8.0, 8.0)
    return whole.astype(jnp.bfloat16)


def block_levels(stream_key, extent, pieces, least, top_value):
    factor_of, own = 1.0, jax.random.fold_in(stream_key, 6)
    for position, shards_of in pieces:
        heights = jnp.exp(jax.random.uniform(jax.random.fold_in(own, position), (shards_of,), jnp.float32, least / len(pieces), top_value / len(pieces)))
        factor_of = factor_of * jnp.repeat(heights, extent[position] // shards_of).reshape([-1 if axis == position else 1 for axis in range(len(extent))])
    return factor_of


def gaussian(rng, dims, spread, limit, pieces=(), kind=jnp.bfloat16):
    values = spread * jax.random.normal(rng, dims, jnp.float32)
    if pieces:
        values = values * block_levels(rng, dims, pieces, -0.22, 0.18)
    return jnp.clip(values, -limit, limit).astype(kind)


def setup_inputs(seed: int = 0) -> dict:
    key_list = jax.random.split(jax.random.key(seed), 5)
    fresh_qkv = draw_fresh_qkv(jax.random.fold_in(key_list[4], 71), 0)
    stale_cache = gaussian(key_list[1], (N_PIPE, TOTAL, 2, WIDTH), 1.75, 8.0, ((0, 32), (3, 8)))
    plan = draw_plan(jax.random.fold_in(key_list[4], 71), 0)
    refresh = draw_refresh(jax.random.fold_in(key_list[4], 71), 0)
    return dict(fresh_qkv=fresh_qkv, stale_cache=stale_cache, plan=plan, refresh=refresh)


def reference(fresh_qkv, stale_cache, plan, refresh):
    fresh = fresh_qkv.reshape(N_PIPE, PT, 3, WIDTH)
    by_patch = jnp.zeros((N_PIPE, PT, 2, WIDTH), fresh_qkv.dtype).at[plan].set(fresh[:, :, 1:3, :])
    patches = jnp.arange(N_PIPE, dtype=jnp.int32)
    factor = 1.0 / math.sqrt(HD)

    def one_section(section):
        own = plan[section]
        listed = refresh[section]
        use = (patches == own) | jnp.any(listed[:, None] == patches[None, :], axis=0)
        cache = stale_cache[section].reshape(N_PIPE, PT, 2, WIDTH)
        keyvalue = jnp.where(use[:, None, None, None], by_patch, cache).reshape(TOTAL, 2, WIDTH)
        query = fresh[section][:, 0, :].astype(jnp.float32).reshape(PT, HEADS, HD)
        keys = keyvalue[:, 0, :].astype(jnp.float32).reshape(TOTAL, HEADS, HD)
        values = keyvalue[:, 1, :].astype(jnp.float32).reshape(TOTAL, HEADS, HD)
        scores = jnp.einsum('qhd,khd->hqk', query, keys) * factor
        top = lax.optimization_barrier(jnp.max(scores, axis=-1, keepdims=True))
        probs = jnp.exp(scores - top)
        totals = lax.optimization_barrier(jnp.sum(probs, axis=-1))
        weights = probs.astype(jnp.bfloat16).astype(jnp.float32)
        mixed = jnp.einsum('hqk,khd->qhd', weights, values) / jnp.transpose(totals)[:, :, None]
        return mixed.reshape(PT, WIDTH).astype(jnp.bfloat16)
    result = lax.map(one_section, jnp.arange(N_PIPE, dtype=jnp.int32))
    return result.reshape(TOTAL, WIDTH)
```

```python
import functools
import math

import jax
import jax.numpy as jnp
from jax import lax
from jax.experimental import pallas as pl
from jax.experimental.pallas import tpu as pltpu
from jax.sharding import PartitionSpec as P

HD = 128
PT = 256
LOCAL = 3
WIDE = LOCAL * HD
PATCHES = 32
SLOTS = 6
SCALE = math.log2(math.e) / math.sqrt(HD)
GROUP = 4
HALF = 16
VMEM_BYTES = 50 * 1024 * 1024


def scores_of(query, keys):
    return lax.dot_general(query, keys, (((1,), (1,)), ((), ())), preferred_element_type=jnp.float32)


def absorb(head, scores, values, top_ref, sum_ref, acc_ref):
    before = top_ref[head]
    top = jnp.maximum(before, jnp.max(scores, axis=1, keepdims=True) * SCALE)
    fade = jnp.exp2(before - top)
    total = sum_ref[head] * fade
    parts = []
    for start in range(0, values.shape[0], HD):
        probs = jnp.exp2(scores[:, start:start + HD] * SCALE - top)
        total = total + probs
        parts.append(probs.astype(jnp.bfloat16))
    weights = jnp.concatenate(parts, axis=1)
    mixed = jnp.dot(weights, values, preferred_element_type=jnp.float32)
    acc_ref[head] = acc_ref[head] * fade + mixed
    sum_ref[head] = total
    top_ref[head] = top


def attend(query_of, keys_of, values_of, state):
    scores = [scores_of(query_of(head), keys_of(head)) for head in range(LOCAL)]
    for head in range(LOCAL):
        absorb(head, scores[head], values_of(head), *state)


def columns(head):
    return slice(head * HD, (head + 1) * HD)


def stale_kernel(least, most, me_ref, plan_ref, refresh_ref, query_ref, cache_ref, *rest):
    taken, state, (held, arrived) = rest[:-5], rest[-5:-2], rest[-2:]
    own = plan_ref[me_ref[0]]
    count = jnp.int32(0)
    for patch in range(PATCHES):
        fresh = own == patch
        for slot in range(SLOTS):
            fresh = jnp.logical_or(fresh, refresh_ref[0, slot] == patch)
        wanted = jnp.logical_not(fresh) & (count >= least) & (count < most)

        @pl.when(wanted)
        def _(patch=patch, place=count - least):
            pltpu.make_async_copy(
                cache_ref.at[:, pl.ds(patch * PT, PT), :], held.at[:, place], arrived.at[place]
            ).start()

        count = count + jnp.where(fresh, 0, 1)
    count = jnp.minimum(count, most) - least
    if taken:
        for source, target in zip(taken, state):
            target[...] = source[...]
    else:
        for target, value in zip(state, (-jnp.inf, 0.0, 0.0)):
            target[...] = jnp.full(target.shape, value, jnp.float32)

    def step(first, width):
        for slot in range(width):
            pltpu.make_async_copy(
                cache_ref.at[:, pl.ds(0, PT), :], held.at[:, first + slot], arrived.at[first + slot]
            ).wait()
        attend(
            lambda head: query_ref[:, :, columns(head)].reshape(PT, HD),
            lambda head: held[0, pl.ds(first, width), :, columns(head)].reshape(width * PT, HD),
            lambda head: held[1, pl.ds(first, width), :, columns(head)].reshape(width * PT, HD),
            state,
        )

    groups = count // GROUP

    @pl.loop(0, groups)
    def _(group):
        step(group * GROUP, GROUP)

    @pl.loop(groups * GROUP, count)
    def _(slot):
        step(slot, 1)


def stale_attention(least, most, me, plan, refresh, query, cache, taken=()):
    state = jax.ShapeDtypeStruct((LOCAL, PT, HD), jnp.float32)
    smem = pl.BlockSpec(memory_space=pltpu.SMEM)
    vmem = pl.BlockSpec(memory_space=pltpu.VMEM)
    keys = (most - least) * PT
    return pl.pallas_call(
        functools.partial(stale_kernel, least, most),
        out_shape=(state, state, state),
        in_specs=[smem, smem, smem, vmem, pl.BlockSpec(memory_space=pl.ANY)] + [vmem] * len(taken),
        out_specs=(vmem, vmem, vmem),
        scratch_shapes=[
            pltpu.VMEM((2, most - least, PT, WIDE), jnp.bfloat16),
            pltpu.SemaphoreType.DMA((most - least,)),
        ],
        compiler_params=pltpu.CompilerParams(vmem_limit_bytes=VMEM_BYTES),
        cost_estimate=pl.CostEstimate(
            flops=8 * LOCAL * PT * keys * HD, bytes_accessed=2 * keys * WIDE * 2, transcendentals=LOCAL * PT * keys
        ),
        name="stale_attention",
    )(me, plan, refresh, query, cache, *taken)


def fresh_kernel(me_ref, plan_ref, refresh_ref, query_ref, top_in, sum_in, acc_in, *rest):
    blocks, (out_ref, top_ref, sum_ref, acc_ref) = rest[:7], rest[7:]
    top_ref[...] = top_in[...]
    sum_ref[...] = sum_in[...]
    acc_ref[...] = acc_in[...]
    me = me_ref[0]

    def step(block):
        attend(
            lambda head: query_ref[:, :, columns(head)].reshape(PT, HD),
            lambda head: block[:, 0, :, columns(head)].reshape(PT, HD),
            lambda head: block[:, 1, :, columns(head)].reshape(PT, HD),
            (top_ref, sum_ref, acc_ref),
        )

    step(blocks[0])
    sections = PATCHES
    even = me % 2 == 0
    sign = jnp.where(even, 1, -1)
    origins = (me - 2, me + 2, me - 3 * sign, me + sign, me + sign - 2, me + sign + 2)
    for origin, block in zip(origins, blocks[1:]):
        patch = plan_ref[(origin + sections) % sections]
        listed = refresh_ref[0, 0] == patch
        for slot in range(1, SLOTS):
            listed = jnp.logical_or(listed, refresh_ref[0, slot] == patch)

        @pl.when(listed)
        def _(block=block):
            step(block)

    for head in range(LOCAL):
        total = jnp.sum(sum_ref[head], axis=1, keepdims=True)
        done = (acc_ref[head] / total).astype(jnp.bfloat16)
        out_ref[:, :, head * HD:(head + 1) * HD] = done.reshape(out_ref.shape[0], out_ref.shape[1], HD)


def fresh_attention(me, plan, refresh, query, state, blocks):
    smem = pl.BlockSpec(memory_space=pltpu.SMEM)
    vmem = pl.BlockSpec(memory_space=pltpu.VMEM)
    held = pltpu.VMEM((LOCAL, PT, HD), jnp.float32)
    return pl.pallas_call(
        fresh_kernel,
        out_shape=jax.ShapeDtypeStruct(query.shape, jnp.bfloat16),
        in_specs=[smem] * 3 + [vmem] * 11,
        out_specs=vmem,
        scratch_shapes=[held, held, held],
        compiler_params=pltpu.CompilerParams(vmem_limit_bytes=32 * 1024 * 1024),
        name="fresh_attention",
    )(me, plan, refresh, query, *state, *blocks)


def move(value, target):
    count = lax.axis_size("pipe")
    return lax.ppermute(value, "pipe", [(source, target(source) % count) for source in range(count)])


def exchange(value):
    return lax.all_to_all(value, "uly", split_axis=0, concat_axis=0, tiled=True)


def shards(fresh_qkv, stale_cache, plan, refresh):
    rows = fresh_qkv.shape[0]
    devices = lax.axis_size("uly")
    me = lax.axis_index("pipe").astype(jnp.int32).reshape(1)
    outgoing = fresh_qkv.reshape(rows, 3, devices, WIDE).transpose(2, 1, 0, 3)
    heads = exchange(outgoing)
    cache = stale_cache[0].transpose(1, 0, 2)
    heads, cache = lax.optimization_barrier((heads, cache))
    own, query = heads[:, 1:3], heads[:, 0]
    behind = move(own, lambda s: s + 2)
    ahead = move(own, lambda s: s - 2)
    far = move(own, lambda s: s + 3 if s % 2 else s - 3)
    twin = lambda s: s ^ 1
    beside = move(own, twin)
    state = stale_attention(0, HALF, me, plan, refresh, query, cache)
    state, behind, ahead = lax.optimization_barrier((state, behind, ahead))
    beside_behind = move(behind, twin)
    beside_ahead = move(ahead, twin)
    state = stale_attention(HALF, PATCHES - 1, me, plan, refresh, query, cache, state)
    blocks = (own, behind, ahead, far, beside, beside_behind, beside_ahead)
    mixed = fresh_attention(me, plan, refresh, query, state, blocks)
    back = exchange(mixed)
    return back.transpose(1, 0, 2).reshape(rows, devices * WIDE)


def solution(mesh):
    placed = (P(("pipe", "uly"), None, None), P("pipe", None, None, "uly"), P(), P("pipe", None))
    return jax.shard_map(
        shards, mesh=mesh, in_specs=placed, out_specs=P(("pipe", "uly"), None), check_vma=False
    )
```

```python
import math

import jax
import jax.numpy as jnp
from jax import lax
from jax.experimental import pallas as pl
from jax.experimental.pallas import tpu as pltpu
from jax.sharding import PartitionSpec as P

HD = 128
PT = 256
LOCAL = 3
WIDE = LOCAL * HD
PATCHES = 32
SLOTS = 6
SCALE = math.log2(math.e) / math.sqrt(HD)
GROUP = 6
FIRST = 24
VMEM_BYTES = 50 * 1024 * 1024


def columns(head):
    return slice(head * HD, (head + 1) * HD)


def absorb(head, scores, values, biases, top_ref, sum_ref, acc_ref):
    before = top_ref[head]
    top = before
    for score, bias in zip(scores, biases):
        widest = score[:, :HD]
        for start in range(HD, PT, HD):
            widest = jnp.maximum(widest, score[:, start:start + HD])
        widest = widest * SCALE
        top = jnp.maximum(top, widest if bias is None else widest + bias)
    top = jnp.broadcast_to(jnp.max(top, axis=1, keepdims=True), top.shape)
    fade = jnp.exp2(before - top)
    total = sum_ref[head] * fade
    mixed = acc_ref[head] * fade
    for score, value, bias in zip(scores, values, biases):
        level = top if bias is None else top - bias
        parts = []
        for start in range(0, PT, HD):
            probs = jnp.exp2(score[:, start:start + HD] * SCALE - level)
            total = total + probs
            parts.append(probs.astype(jnp.bfloat16))
        weights = jnp.concatenate(parts, axis=1)
        mixed = mixed + jnp.dot(weights, value, preferred_element_type=jnp.float32)
    acc_ref[head] = mixed
    sum_ref[head] = total
    top_ref[head] = top


def attend(query_ref, readers, biases, state):
    scores = []
    for head in range(LOCAL):
        query = query_ref[:, :, columns(head)].reshape(PT, HD)
        scores.append([
            lax.dot_general(query, read(0, head), (((1,), (1,)), ((), ())), preferred_element_type=jnp.float32)
            for read in readers
        ])
    for head in range(LOCAL):
        absorb(head, scores[head], [read(1, head) for read in readers], biases, *state)


def cached(held, place):
    return lambda part, head: held[part, place, :, columns(head)]


def moved(block_ref):
    return lambda part, head: block_ref[:, part, :, columns(head)].reshape(PT, HD)


def listing(patch, refresh_ref):
    found = refresh_ref[0, 0] == patch
    for slot in range(1, SLOTS):
        found = jnp.logical_or(found, refresh_ref[0, slot] == patch)
    return found


def bias_of(section, plan_ref, refresh_ref):
    patch = plan_ref[(section + PATCHES) % PATCHES]
    return jnp.where(listing(patch, refresh_ref), 0.0, -jnp.inf).astype(jnp.float32)


def fetch_stale(least, most, me_ref, plan_ref, refresh_ref, cache_ref, held, arrived):
    own = plan_ref[me_ref[0]]
    count = jnp.int32(0)
    for patch in range(PATCHES):
        stale = jnp.logical_not(jnp.logical_or(own == patch, listing(patch, refresh_ref)))

        @pl.when(stale & (count >= least) & (count < most))
        def _(patch=patch, place=count - least):
            pltpu.make_async_copy(
                cache_ref.at[:, pl.ds(patch * PT, PT), :], held.at[:, place], arrived.at[place]
            ).start()

        count = count + jnp.where(stale, 1, 0)
    return count


def attend_stale(first, width, query_ref, cache_ref, held, arrived, state):
    for place in range(width):
        pltpu.make_async_copy(
            cache_ref.at[:, pl.ds(0, PT), :], held.at[:, first + place], arrived.at[first + place]
        ).wait()
    attend(query_ref, [cached(held, first + place) for place in range(width)], [None] * width, state)


def sign_of(me):
    return jnp.where(me % 2 == 0, 1, -1)


def first_kernel(me_ref, plan_ref, refresh_ref, cache_ref, query_ref, top_ref, sum_ref, acc_ref, held, arrived):
    fetch_stale(0, FIRST, me_ref, plan_ref, refresh_ref, cache_ref, held, arrived)
    state = (top_ref, sum_ref, acc_ref)
    for target, value in zip(state, (-jnp.inf, 0.0, 0.0)):
        target[...] = jnp.full(target.shape, value, jnp.float32)

    @pl.loop(0, FIRST // GROUP)
    def _(group):
        attend_stale(group * GROUP, GROUP, query_ref, cache_ref, held, arrived, state)


def second_kernel(me_ref, plan_ref, refresh_ref, cache_ref, query_ref, top_in, sum_in, acc_in, own_ref, beside_ref,
                  behind_ref, ahead_ref, top_ref, sum_ref, acc_ref, held, arrived):
    left = fetch_stale(FIRST, PATCHES - 1, me_ref, plan_ref, refresh_ref, cache_ref, held, arrived) - FIRST
    state = (top_ref, sum_ref, acc_ref)
    for source, target in zip((top_in, sum_in, acc_in), state):
        target[...] = source[...]
    me = me_ref[0]
    biases = [None] + [
        bias_of(section, plan_ref, refresh_ref) for section in (me + sign_of(me), me - 2, me + 2)
    ]
    readers = [moved(block) for block in (own_ref, beside_ref, behind_ref, ahead_ref)]
    attend(query_ref, readers, biases, state)

    @pl.when(left >= 4)
    def _():
        attend_stale(0, 4, query_ref, cache_ref, held, arrived, state)

    done = jnp.where(left >= 4, 4, 0)
    for width in range(1, 4):

        @pl.when(left - done == width)
        def _(width=width):
            attend_stale(done, width, query_ref, cache_ref, held, arrived, state)


def last_kernel(me_ref, plan_ref, refresh_ref, query_ref, top_in, sum_in, acc_in, far_ref, beside_behind_ref,
                beside_ahead_ref, out_ref, top_ref, sum_ref, acc_ref):
    state = (top_ref, sum_ref, acc_ref)
    for source, target in zip((top_in, sum_in, acc_in), state):
        target[...] = source[...]
    me = me_ref[0]
    sign = sign_of(me)
    biases = [
        bias_of(section, plan_ref, refresh_ref) for section in (me - 3 * sign, me + sign - 2, me + sign + 2)
    ]
    readers = [moved(block) for block in (far_ref, beside_behind_ref, beside_ahead_ref)]
    attend(query_ref, readers, biases, state)
    for head in range(LOCAL):
        total = jnp.sum(sum_ref[head], axis=1, keepdims=True)
        done = (acc_ref[head] / total).astype(jnp.bfloat16)
        out_ref[:, :, columns(head)] = done.reshape(out_ref.shape[0], out_ref.shape[1], HD)


SMEM_SPEC = pl.BlockSpec(memory_space=pltpu.SMEM)
VMEM_SPEC = pl.BlockSpec(memory_space=pltpu.VMEM)
STATE = (jax.ShapeDtypeStruct((LOCAL, PT, HD), jnp.float32),) * 3


def patches(count):
    return [pltpu.VMEM((2, count, PT, WIDE), jnp.bfloat16), pltpu.SemaphoreType.DMA((count,))]


def run(kernel, blocks, scalars, arrays, out_shape, scratch, cache=()):
    keys = blocks * PT
    return pl.pallas_call(
        kernel,
        out_shape=out_shape,
        in_specs=[SMEM_SPEC] * len(scalars) + [pl.BlockSpec(memory_space=pl.ANY)] * len(cache) + [VMEM_SPEC] * len(arrays),
        out_specs=jax.tree.map(lambda _: VMEM_SPEC, out_shape),
        scratch_shapes=scratch,
        compiler_params=pltpu.CompilerParams(vmem_limit_bytes=VMEM_BYTES),
        cost_estimate=pl.CostEstimate(
            flops=8 * LOCAL * PT * keys * HD, bytes_accessed=2 * keys * WIDE * 2, transcendentals=LOCAL * PT * keys
        ),
    )(*scalars, *cache, *arrays)


def move(value, target):
    count = lax.axis_size("pipe")
    return lax.ppermute(value, "pipe", [(source, target(source) % count) for source in range(count)])


def exchange(value):
    return lax.all_to_all(value, "uly", split_axis=0, concat_axis=0, tiled=True)


def shards(fresh_qkv, stale_cache, plan, refresh):
    rows = fresh_qkv.shape[0]
    devices = lax.axis_size("uly")
    me = lax.axis_index("pipe").astype(jnp.int32)
    scalars = (me.reshape(1), plan, refresh)
    outgoing = fresh_qkv.reshape(rows, 3, devices, WIDE).transpose(2, 1, 0, 3)
    heads = exchange(outgoing)
    cache = stale_cache[0].transpose(1, 0, 2)
    heads, cache = lax.optimization_barrier((heads, cache))
    own, query = heads[:, 1:3], heads[:, 0]
    twin = lambda s: s ^ 1
    behind = move(own, lambda s: s + 2)
    ahead = move(own, lambda s: s - 2)
    beside = move(own, twin)
    state = run(first_kernel, FIRST, scalars, (query,), STATE, patches(FIRST), (cache,))
    state, behind, ahead = lax.optimization_barrier((state, behind, ahead))
    beside_behind = move(behind, twin)
    beside_ahead = move(ahead, twin)
    far = move(jnp.where(me % 2 == 1, behind, ahead), lambda s: s + 1 if s % 2 else s - 1)
    state = run(
        second_kernel, 8, scalars, (query, *state, own, beside, behind, ahead), STATE,
        patches(PATCHES - 1 - FIRST), (cache,),
    )
    held = pltpu.VMEM((LOCAL, PT, HD), jnp.float32)
    mixed = run(
        last_kernel, 3, scalars, (query, *state, far, beside_behind, beside_ahead),
        jax.ShapeDtypeStruct(query.shape, jnp.bfloat16), [held] * 3,
    )
    back = exchange(mixed)
    return back.transpose(1, 0, 2).reshape(rows, devices * WIDE)


def solution(mesh):
    placed = (P(("pipe", "uly"), None, None), P("pipe", None, None, "uly"), P(), P("pipe", None))
    return jax.shard_map(
        shards, mesh=mesh, in_specs=placed, out_specs=P(("pipe", "uly"), None), check_vma=False
    )
```

```python
import math

import jax
import jax.numpy as jnp
from jax import lax
from jax.experimental import pallas as pl
from jax.experimental.pallas import tpu as pltpu
from jax.sharding import PartitionSpec as P

HD = 128
PT = 256
LOCAL = 3
WIDE = LOCAL * HD
PATCHES = 32
SLOTS = 6
SCALE = math.log2(math.e) / math.sqrt(HD)
GROUP = 6
FIRST = 24
VMEM_BYTES = 50 * 1024 * 1024


def columns(head):
    return slice(head * HD, (head + 1) * HD)


def absorb(head, scores, values, biases, top_ref, sum_ref, acc_ref):
    before = top_ref[head]
    top = before
    for score, bias in zip(scores, biases):
        widest = score[:, :HD]
        for start in range(HD, PT, HD):
            widest = jnp.maximum(widest, score[:, start:start + HD])
        widest = widest * SCALE
        top = jnp.maximum(top, widest if bias is None else widest + bias)
    top = jnp.broadcast_to(jnp.max(top, axis=1, keepdims=True), top.shape)
    fade = jnp.exp2(before - top)
    total = sum_ref[head] * fade
    mixed = acc_ref[head] * fade
    for score, value, bias in zip(scores, values, biases):
        level = top if bias is None else top - bias
        parts = []
        for start in range(0, PT, HD):
            probs = jnp.exp2(score[:, start:start + HD] * SCALE - level)
            total = total + probs
            parts.append(probs.astype(jnp.bfloat16))
        weights = jnp.concatenate(parts, axis=1)
        mixed = mixed + jnp.dot(weights, value, preferred_element_type=jnp.float32)
    acc_ref[head] = mixed
    sum_ref[head] = total
    top_ref[head] = top


def attend(query_ref, readers, biases, state):
    scores = []
    for head in range(LOCAL):
        query = query_ref[:, :, columns(head)].reshape(PT, HD)
        scores.append([
            lax.dot_general(query, read(0, head), (((1,), (1,)), ((), ())), preferred_element_type=jnp.float32)
            for read in readers
        ])
    for head in range(LOCAL):
        absorb(head, scores[head], [read(1, head) for read in readers], biases, *state)


def cached(held, place):
    return lambda part, head: held[part, place, :, columns(head)]


def moved(block_ref):
    return lambda part, head: block_ref[:, part, :, columns(head)].reshape(PT, HD)


def listing(patch, refresh_ref):
    found = refresh_ref[0, 0] == patch
    for slot in range(1, SLOTS):
        found = jnp.logical_or(found, refresh_ref[0, slot] == patch)
    return found


def bias_of(section, plan_ref, refresh_ref):
    patch = plan_ref[(section + PATCHES) % PATCHES]
    return jnp.where(listing(patch, refresh_ref), 0.0, -jnp.inf).astype(jnp.float32)


def fetch(patch, place, cache_ref, held, arrived):
    return pltpu.make_async_copy(
        cache_ref.at[:, pl.ds(pl.multiple_of(patch * PT, PT), PT), :], held.at[:, place], arrived.at[place]
    )


def attend_stale(first, width, query_ref, cache_ref, held, arrived, state):
    for place in range(width):
        fetch(0, first + place, cache_ref, held, arrived).wait()
    attend(query_ref, [cached(held, first + place) for place in range(width)], [None] * width, state)


def sign_of(me):
    return jnp.where(me % 2 == 0, 1, -1)


def order_kernel(me_ref, plan_ref, refresh_ref, order_ref):
    own = plan_ref[me_ref[0]]
    count = jnp.int32(0)
    for patch in range(PATCHES):
        order_ref[count] = jnp.int32(patch)
        fresh = jnp.logical_or(own == patch, listing(patch, refresh_ref))
        count = count + jnp.where(fresh, 0, 1)
    order_ref[PATCHES] = count


def first_kernel(order_ref, cache_ref, query_ref, top_ref, sum_ref, acc_ref, held, arrived):
    def begin(group):
        for place in range(GROUP):
            place = group * GROUP + place
            fetch(order_ref[place], place, cache_ref, held, arrived).start()

    begin(0)
    begin(1)
    state = (top_ref, sum_ref, acc_ref)
    for target, value in zip(state, (-jnp.inf, 0.0, 0.0)):
        target[...] = jnp.full(target.shape, value, jnp.float32)

    @pl.loop(0, FIRST // GROUP)
    def _(group):
        @pl.when(group + 2 < FIRST // GROUP)
        def _():
            begin(group + 2)

        attend_stale(group * GROUP, GROUP, query_ref, cache_ref, held, arrived, state)


def second_kernel(me_ref, plan_ref, refresh_ref, order_ref, cache_ref, query_ref, top_in, sum_in, acc_in, own_ref,
                  beside_ref, behind_ref, ahead_ref, top_ref, sum_ref, acc_ref, held, arrived):
    left = order_ref[PATCHES] - FIRST

    @pl.loop(0, left)
    def _(place):
        fetch(order_ref[FIRST + place], place, cache_ref, held, arrived).start()

    state = (top_ref, sum_ref, acc_ref)
    for source, target in zip((top_in, sum_in, acc_in), state):
        target[...] = source[...]
    me = me_ref[0]
    biases = [None] + [
        bias_of(section, plan_ref, refresh_ref) for section in (me + sign_of(me), me - 2, me + 2)
    ]
    readers = [moved(block) for block in (own_ref, beside_ref, behind_ref, ahead_ref)]
    attend(query_ref, readers, biases, state)

    @pl.when(left >= 4)
    def _():
        attend_stale(0, 4, query_ref, cache_ref, held, arrived, state)

    done = jnp.where(left >= 4, 4, 0)
    for width in range(1, 4):

        @pl.when(left - done == width)
        def _(width=width):
            attend_stale(done, width, query_ref, cache_ref, held, arrived, state)


def last_kernel(me_ref, plan_ref, refresh_ref, query_ref, top_in, sum_in, acc_in, far_ref, beside_behind_ref,
                beside_ahead_ref, out_ref, top_ref, sum_ref, acc_ref):
    state = (top_ref, sum_ref, acc_ref)
    for source, target in zip((top_in, sum_in, acc_in), state):
        target[...] = source[...]
    me = me_ref[0]
    sign = sign_of(me)
    biases = [
        bias_of(section, plan_ref, refresh_ref) for section in (me - 3 * sign, me + sign - 2, me + sign + 2)
    ]
    readers = [moved(block) for block in (far_ref, beside_behind_ref, beside_ahead_ref)]
    attend(query_ref, readers, biases, state)
    for head in range(LOCAL):
        total = jnp.sum(sum_ref[head], axis=1, keepdims=True)
        done = (acc_ref[head] / total).astype(jnp.bfloat16)
        out_ref[:, :, columns(head)] = done.reshape(out_ref.shape[0], out_ref.shape[1], HD)


SMEM_SPEC = pl.BlockSpec(memory_space=pltpu.SMEM)
VMEM_SPEC = pl.BlockSpec(memory_space=pltpu.VMEM)
STATE = (jax.ShapeDtypeStruct((LOCAL, PT, HD), jnp.float32),) * 3


def patches(count):
    return [pltpu.VMEM((2, count, PT, WIDE), jnp.bfloat16), pltpu.SemaphoreType.DMA((count,))]


def run(kernel, blocks, scalars, arrays, out_shape, scratch, cache=()):
    keys = blocks * PT
    return pl.pallas_call(
        kernel,
        out_shape=out_shape,
        in_specs=[SMEM_SPEC] * len(scalars) + [pl.BlockSpec(memory_space=pl.ANY)] * len(cache) + [VMEM_SPEC] * len(arrays),
        out_specs=jax.tree.map(lambda _: VMEM_SPEC, out_shape),
        scratch_shapes=scratch,
        compiler_params=pltpu.CompilerParams(vmem_limit_bytes=VMEM_BYTES),
        cost_estimate=pl.CostEstimate(
            flops=8 * LOCAL * PT * keys * HD, bytes_accessed=2 * keys * WIDE * 2, transcendentals=LOCAL * PT * keys
        ),
    )(*scalars, *cache, *arrays)


def stale_order(scalars):
    return pl.pallas_call(
        order_kernel,
        out_shape=jax.ShapeDtypeStruct((PATCHES + 1,), jnp.int32),
        in_specs=[SMEM_SPEC] * 3,
        out_specs=SMEM_SPEC,
    )(*scalars)


def move(value, target):
    count = lax.axis_size("pipe")
    return lax.ppermute(value, "pipe", [(source, target(source) % count) for source in range(count)])


def exchange(value):
    return lax.all_to_all(value, "uly", split_axis=0, concat_axis=0, tiled=True)


def shards(fresh_qkv, stale_cache, plan, refresh):
    rows = fresh_qkv.shape[0]
    devices = lax.axis_size("uly")
    me = lax.axis_index("pipe").astype(jnp.int32)
    scalars = (me.reshape(1), plan, refresh)
    outgoing = fresh_qkv.reshape(rows, 3, devices, WIDE).transpose(2, 1, 0, 3)
    heads = exchange(outgoing)
    cache = stale_cache[0].transpose(1, 0, 2)
    order = stale_order(scalars)
    heads, cache, order = lax.optimization_barrier((heads, cache, order))
    own, query = heads[:, 1:3], heads[:, 0]
    twin = lambda s: s ^ 1
    behind = move(own, lambda s: s + 2)
    ahead = move(own, lambda s: s - 2)
    beside = move(own, twin)
    state = run(first_kernel, FIRST, (order,), (query,), STATE, patches(FIRST), (cache,))
    state, behind, ahead = lax.optimization_barrier((state, behind, ahead))
    beside_behind = move(behind, twin)
    beside_ahead = move(ahead, twin)
    far = move(jnp.where(me % 2 == 1, behind, ahead), lambda s: s + 1 if s % 2 else s - 1)
    state = run(
        second_kernel, 8, (*scalars, order), (query, *state, own, beside, behind, ahead), STATE,
        patches(PATCHES - 1 - FIRST), (cache,),
    )
    held = pltpu.VMEM((LOCAL, PT, HD), jnp.float32)
    mixed = run(
        last_kernel, 3, scalars, (query, *state, far, beside_behind, beside_ahead),
        jax.ShapeDtypeStruct(query.shape, jnp.bfloat16), [held] * 3,
    )
    back = exchange(mixed)
    return back.transpose(1, 0, 2).reshape(rows, devices * WIDE)


def solution(mesh):
    placed = (P(("pipe", "uly"), None, None), P("pipe", None, None, "uly"), P(), P("pipe", None))
    return jax.shard_map(
        shards, mesh=mesh, in_specs=placed, out_specs=P(("pipe", "uly"), None), check_vma=False
    )
```

```python
import math

import jax
import jax.numpy as jnp
from jax import lax
from jax.experimental import pallas as pl
from jax.experimental.pallas import tpu as pltpu
from jax.sharding import PartitionSpec as P

HD = 128
PT = 256
LOCAL = 3
WIDE = LOCAL * HD
PATCHES = 32
SLOTS = 6
SCALE = math.log2(math.e) / math.sqrt(HD)
GROUP = 6
FIRST = 24
VMEM_BYTES = 48 * 1024 * 1024


def columns(head):
    return slice(head * HD, (head + 1) * HD)


def absorb(head, scores, values, biases, top_ref, sum_ref, acc_ref):
    before = top_ref[head]
    top = before
    for score, bias in zip(scores, biases):
        widest = score[:, :HD]
        for start in range(HD, PT, HD):
            widest = jnp.maximum(widest, score[:, start:start + HD])
        widest = widest * SCALE
        top = jnp.maximum(top, widest if bias is None else widest + bias)
    top = jnp.broadcast_to(jnp.max(top, axis=1, keepdims=True), top.shape)
    fade = jnp.exp2(before - top)
    total = sum_ref[head] * fade
    mixed = acc_ref[head] * fade
    for score, value, bias in zip(scores, values, biases):
        level = top if bias is None else top - bias
        parts = []
        for start in range(0, PT, HD):
            probs = jnp.exp2(score[:, start:start + HD] * SCALE - level)
            total = total + probs
            parts.append(probs.astype(jnp.bfloat16))
        weights = jnp.concatenate(parts, axis=1)
        mixed = mixed + jnp.dot(weights, value, preferred_element_type=jnp.float32)
    acc_ref[head] = mixed
    sum_ref[head] = total
    top_ref[head] = top


def attend(query_ref, readers, biases, state):
    scores = []
    for head in range(LOCAL):
        query = query_ref[:, :, columns(head)].reshape(PT, HD)
        scores.append([
            lax.dot_general(query, read(0, head), (((1,), (1,)), ((), ())), preferred_element_type=jnp.float32)
            for read in readers
        ])
    for head in range(LOCAL):
        absorb(head, scores[head], [read(1, head) for read in readers], biases, *state)


def cached(held, place):
    return lambda part, head: held[part, place, :, columns(head)]


def moved(block_ref):
    return lambda part, head: block_ref[:, part, :, columns(head)].reshape(PT, HD)


def listing(patch, refresh_ref):
    found = refresh_ref[0, 0] == patch
    for slot in range(1, SLOTS):
        found = jnp.logical_or(found, refresh_ref[0, slot] == patch)
    return found


def bias_of(section, plan_ref, refresh_ref):
    patch = plan_ref[(section + PATCHES) % PATCHES]
    return jnp.where(listing(patch, refresh_ref), 0.0, -jnp.inf).astype(jnp.float32)


def fetch(patch, place, cache_ref, held, arrived):
    return pltpu.make_async_copy(
        cache_ref.at[:, pl.ds(pl.multiple_of(patch * PT, PT), PT), :], held.at[:, place], arrived.at[place]
    )


def attend_stale(first, width, query_ref, cache_ref, held, arrived, state):
    for place in range(width):
        fetch(0, first + place, cache_ref, held, arrived).wait()
    attend(query_ref, [cached(held, first + place) for place in range(width)], [None] * width, state)


def sign_of(me):
    return jnp.where(me % 2 == 0, 1, -1)


def order_kernel(me_ref, plan_ref, refresh_ref, cache_ref, order_ref, early, arrived):
    one = jnp.int32(1)
    fresh = jnp.left_shift(one, plan_ref[me_ref[0]])
    for slot in range(SLOTS):
        patch = refresh_ref[0, slot]
        fresh = fresh | jnp.where(patch >= 0, jnp.left_shift(one, jnp.maximum(patch, 0)), 0)
    count = jnp.int32(0)
    for patch in range(PATCHES):
        order_ref[count] = jnp.int32(patch)
        count = count + 1 - (jnp.right_shift(fresh, patch) & 1)
    order_ref[PATCHES] = count
    copies = [fetch(order_ref[place], place, cache_ref, early, arrived) for place in range(GROUP)]
    for copy in copies:
        copy.start()
    for copy in copies:
        copy.wait()


def first_kernel(order_ref, cache_ref, query_ref, early, top_ref, sum_ref, acc_ref, held, arrived):
    def begin(group):
        for place in range(GROUP):
            place = group * GROUP + place
            fetch(order_ref[GROUP + place], place, cache_ref, held, arrived).start()

    begin(0)
    begin(1)
    state = (top_ref, sum_ref, acc_ref)
    for target, value in zip(state, (-jnp.inf, 0.0, 0.0)):
        target[...] = jnp.full(target.shape, value, jnp.float32)
    attend(query_ref, [cached(early, place) for place in range(GROUP)], [None] * GROUP, state)

    @pl.loop(0, FIRST // GROUP - 1)
    def _(group):
        @pl.when(group + 2 < FIRST // GROUP - 1)
        def _():
            begin(group + 2)

        attend_stale(group * GROUP, GROUP, query_ref, cache_ref, held, arrived, state)


def second_kernel(me_ref, plan_ref, refresh_ref, order_ref, cache_ref, query_ref, top_in, sum_in, acc_in, own_ref,
                  beside_ref, behind_ref, ahead_ref, top_ref, sum_ref, acc_ref, held, arrived):
    left = order_ref[PATCHES] - FIRST

    @pl.loop(0, left)
    def _(place):
        fetch(order_ref[FIRST + place], place, cache_ref, held, arrived).start()

    state = (top_ref, sum_ref, acc_ref)
    for source, target in zip((top_in, sum_in, acc_in), state):
        target[...] = source[...]
    me = me_ref[0]
    biases = [None] + [
        bias_of(section, plan_ref, refresh_ref) for section in (me + sign_of(me), me - 2, me + 2)
    ]
    readers = [moved(block) for block in (own_ref, beside_ref, behind_ref, ahead_ref)]
    attend(query_ref, readers, biases, state)

    @pl.when(left >= 4)
    def _():
        attend_stale(0, 4, query_ref, cache_ref, held, arrived, state)

    done = jnp.where(left >= 4, 4, 0)
    for width in range(1, 4):

        @pl.when(left - done == width)
        def _(width=width):
            attend_stale(done, width, query_ref, cache_ref, held, arrived, state)


def last_kernel(me_ref, plan_ref, refresh_ref, query_ref, top_in, sum_in, acc_in, far_ref, beside_behind_ref,
                beside_ahead_ref, out_ref, top_ref, sum_ref, acc_ref):
    state = (top_ref, sum_ref, acc_ref)
    for source, target in zip((top_in, sum_in, acc_in), state):
        target[...] = source[...]
    me = me_ref[0]
    sign = sign_of(me)
    biases = [
        bias_of(section, plan_ref, refresh_ref) for section in (me - 3 * sign, me + sign - 2, me + sign + 2)
    ]
    readers = [moved(block) for block in (far_ref, beside_behind_ref, beside_ahead_ref)]
    attend(query_ref, readers, biases, state)
    for head in range(LOCAL):
        total = jnp.sum(sum_ref[head], axis=1, keepdims=True)
        done = (acc_ref[head] / total).astype(jnp.bfloat16)
        out_ref[:, :, columns(head)] = done.reshape(out_ref.shape[0], out_ref.shape[1], HD)


SMEM_SPEC = pl.BlockSpec(memory_space=pltpu.SMEM)
VMEM_SPEC = pl.BlockSpec(memory_space=pltpu.VMEM)
STATE = (jax.ShapeDtypeStruct((LOCAL, PT, HD), jnp.float32),) * 3


def patches(count):
    return [pltpu.VMEM((2, count, PT, WIDE), jnp.bfloat16), pltpu.SemaphoreType.DMA((count,))]


def run(kernel, blocks, scalars, arrays, out_shape, scratch, cache=()):
    keys = blocks * PT
    return pl.pallas_call(
        kernel,
        out_shape=out_shape,
        in_specs=[SMEM_SPEC] * len(scalars) + [pl.BlockSpec(memory_space=pl.ANY)] * len(cache) + [VMEM_SPEC] * len(arrays),
        out_specs=jax.tree.map(lambda _: VMEM_SPEC, out_shape),
        scratch_shapes=scratch,
        compiler_params=pltpu.CompilerParams(vmem_limit_bytes=VMEM_BYTES),
        cost_estimate=pl.CostEstimate(
            flops=8 * LOCAL * PT * keys * HD, bytes_accessed=2 * keys * WIDE * 2, transcendentals=LOCAL * PT * keys
        ),
    )(*scalars, *cache, *arrays)


def stale_order(scalars, cache):
    return pl.pallas_call(
        order_kernel,
        out_shape=(
            jax.ShapeDtypeStruct((PATCHES + 1,), jnp.int32), jax.ShapeDtypeStruct((2, GROUP, PT, WIDE), cache.dtype)
        ),
        in_specs=[SMEM_SPEC] * 3 + [pl.BlockSpec(memory_space=pl.ANY)],
        out_specs=(SMEM_SPEC, VMEM_SPEC),
        scratch_shapes=[pltpu.SemaphoreType.DMA((GROUP,))],
        compiler_params=pltpu.CompilerParams(vmem_limit_bytes=VMEM_BYTES),
    )(*scalars, cache)


def move(value, target):
    count = lax.axis_size("pipe")
    return lax.ppermute(value, "pipe", [(source, target(source) % count) for source in range(count)])


def exchange(value):
    return lax.all_to_all(value, "uly", split_axis=0, concat_axis=0, tiled=True)


def shards(fresh_qkv, stale_cache, plan, refresh):
    rows = fresh_qkv.shape[0]
    devices = lax.axis_size("uly")
    me = lax.axis_index("pipe").astype(jnp.int32)
    scalars = (me.reshape(1), plan, refresh)
    outgoing = fresh_qkv.reshape(rows, 3, devices, WIDE).transpose(2, 1, 0, 3)
    heads = exchange(outgoing)
    cache = stale_cache[0].transpose(1, 0, 2)
    order, early = stale_order(scalars, cache)
    heads, cache, order, early = lax.optimization_barrier((heads, cache, order, early))
    own, query = heads[:, 1:3], heads[:, 0]
    twin = lambda s: s ^ 1
    behind = move(own, lambda s: s + 2)
    ahead = move(own, lambda s: s - 2)
    beside = move(own, twin)
    state = run(first_kernel, FIRST, (order,), (query, early), STATE, patches(FIRST - GROUP), (cache,))
    state, behind, ahead = lax.optimization_barrier((state, behind, ahead))
    beside_behind = move(behind, twin)
    beside_ahead = move(ahead, twin)
    far = move(jnp.where(me % 2 == 1, behind, ahead), lambda s: s + 1 if s % 2 else s - 1)
    state = run(
        second_kernel, 8, (*scalars, order), (query, *state, own, beside, behind, ahead), STATE,
        patches(PATCHES - 1 - FIRST), (cache,),
    )
    held = pltpu.VMEM((LOCAL, PT, HD), jnp.float32)
    mixed = run(
        last_kernel, 3, scalars, (query, *state, far, beside_behind, beside_ahead),
        jax.ShapeDtypeStruct(query.shape, jnp.bfloat16), [held] * 3,
    )
    back = exchange(mixed)
    return back.transpose(1, 0, 2).reshape(rows, devices * WIDE)


def solution(mesh):
    placed = (P(("pipe", "uly"), None, None), P("pipe", None, None, "uly"), P(), P("pipe", None))
    return jax.shard_map(
        shards, mesh=mesh, in_specs=placed, out_specs=P(("pipe", "uly"), None), check_vma=False
    )
```

```python
import math

import jax
import jax.numpy as jnp
from jax import lax
from jax.experimental import pallas as pl
from jax.experimental.pallas import tpu as pltpu
from jax.sharding import PartitionSpec as P

HD = 128
PT = 256
LOCAL = 3
WIDE = LOCAL * HD
PATCHES = 32
SLOTS = 6
SCALE = math.log2(math.e) / math.sqrt(HD)
GROUP = 6
FIRST = 24
VMEM_BYTES = 48 * 1024 * 1024


def columns(head):
    return slice(head * HD, (head + 1) * HD)


def absorb(head, scores, values, biases, top_ref, sum_ref, acc_ref):
    before = top_ref[head]
    top = before
    for score, bias in zip(scores, biases):
        widest = score[:, :HD]
        for start in range(HD, PT, HD):
            widest = jnp.maximum(widest, score[:, start:start + HD])
        widest = widest * SCALE
        top = jnp.maximum(top, widest if bias is None else widest + bias)
    top = jnp.broadcast_to(jnp.max(top, axis=1, keepdims=True), top.shape)
    fade = jnp.exp2(before - top)
    total = sum_ref[head] * fade
    mixed = acc_ref[head] * fade
    for score, value, bias in zip(scores, values, biases):
        level = top if bias is None else top - bias
        parts = []
        for start in range(0, PT, HD):
            probs = jnp.exp2(score[:, start:start + HD] * SCALE - level)
            total = total + probs
            parts.append(probs.astype(jnp.bfloat16))
        weights = jnp.concatenate(parts, axis=1)
        mixed = mixed + jnp.dot(weights, value, preferred_element_type=jnp.float32)
    return top, total, mixed


def absorbed(query_ref, readers, biases, source):
    scores = []
    for head in range(LOCAL):
        query = query_ref[:, :, columns(head)].reshape(PT, HD)
        scores.append([
            lax.dot_general(query, read(0, head), (((1,), (1,)), ((), ())), preferred_element_type=jnp.float32)
            for read in readers
        ])
    for head in range(LOCAL):
        yield head, absorb(head, scores[head], [read(1, head) for read in readers], biases, *source)


def attend(query_ref, readers, biases, state, source=None):
    top_ref, sum_ref, acc_ref = state
    for head, (top, total, mixed) in absorbed(query_ref, readers, biases, source or state):
        acc_ref[head] = mixed
        sum_ref[head] = total
        top_ref[head] = top


def cached(held, place):
    return lambda part, head: held[part, place, :, columns(head)]


def moved(block_ref):
    return lambda part, head: block_ref[:, part, :, columns(head)].reshape(PT, HD)


def listing(patch, refresh_ref):
    found = refresh_ref[0, 0] == patch
    for slot in range(1, SLOTS):
        found = jnp.logical_or(found, refresh_ref[0, slot] == patch)
    return found


def bias_of(section, plan_ref, refresh_ref):
    patch = plan_ref[(section + PATCHES) % PATCHES]
    return jnp.where(listing(patch, refresh_ref), 0.0, -jnp.inf).astype(jnp.float32)


def fetch(patch, place, cache_ref, held, arrived):
    return pltpu.make_async_copy(
        cache_ref.at[:, pl.ds(pl.multiple_of(patch * PT, PT), PT), :], held.at[:, place], arrived.at[place]
    )


def attend_stale(first, width, query_ref, cache_ref, held, arrived, state):
    for place in range(width):
        fetch(0, first + place, cache_ref, held, arrived).wait()
    attend(query_ref, [cached(held, first + place) for place in range(width)], [None] * width, state)


def sign_of(me):
    return jnp.where(me % 2 == 0, 1, -1)


def order_kernel(me_ref, plan_ref, refresh_ref, cache_ref, order_ref, early, arrived):
    one = jnp.int32(1)
    fresh = jnp.left_shift(one, plan_ref[me_ref[0]])
    for slot in range(SLOTS):
        patch = refresh_ref[0, slot]
        fresh = fresh | jnp.where(patch >= 0, jnp.left_shift(one, jnp.maximum(patch, 0)), 0)
    count = jnp.int32(0)
    for patch in range(PATCHES):
        order_ref[count] = jnp.int32(patch)
        count = count + 1 - (jnp.right_shift(fresh, patch) & 1)
    order_ref[PATCHES] = count
    copies = [fetch(order_ref[place], place, cache_ref, early, arrived) for place in range(GROUP)]
    for copy in copies:
        copy.start()
    for copy in copies:
        copy.wait()


def first_kernel(order_ref, cache_ref, query_ref, early, top_ref, sum_ref, acc_ref, held, arrived):
    def begin(group):
        for place in range(GROUP):
            place = group * GROUP + place
            fetch(order_ref[GROUP + place], place, cache_ref, held, arrived).start()

    begin(0)
    begin(1)
    state = (top_ref, sum_ref, acc_ref)
    for target, value in zip(state, (-jnp.inf, 0.0, 0.0)):
        target[...] = jnp.full(target.shape, value, jnp.float32)
    attend(query_ref, [cached(early, place) for place in range(GROUP)], [None] * GROUP, state)

    @pl.loop(0, FIRST // GROUP - 1)
    def _(group):
        @pl.when(group + 2 < FIRST // GROUP - 1)
        def _():
            begin(group + 2)

        attend_stale(group * GROUP, GROUP, query_ref, cache_ref, held, arrived, state)


def second_kernel(me_ref, plan_ref, refresh_ref, order_ref, cache_ref, query_ref, top_in, sum_in, acc_in, own_ref,
                  beside_ref, behind_ref, ahead_ref, top_ref, sum_ref, acc_ref, held, arrived):
    left = order_ref[PATCHES] - FIRST

    @pl.loop(0, left)
    def _(place):
        fetch(order_ref[FIRST + place], place, cache_ref, held, arrived).start()

    state = (top_ref, sum_ref, acc_ref)
    me = me_ref[0]
    biases = [None] + [
        bias_of(section, plan_ref, refresh_ref) for section in (me + sign_of(me), me - 2, me + 2)
    ]
    readers = [moved(block) for block in (own_ref, beside_ref, behind_ref, ahead_ref)]
    attend(query_ref, readers, biases, state, (top_in, sum_in, acc_in))

    @pl.when(left >= 4)
    def _():
        attend_stale(0, 4, query_ref, cache_ref, held, arrived, state)

    done = jnp.where(left >= 4, 4, 0)
    for width in range(1, 4):

        @pl.when(left - done == width)
        def _(width=width):
            attend_stale(done, width, query_ref, cache_ref, held, arrived, state)


def last_kernel(me_ref, plan_ref, refresh_ref, query_ref, top_in, sum_in, acc_in, far_ref, beside_behind_ref,
                beside_ahead_ref, out_ref):
    me = me_ref[0]
    sign = sign_of(me)
    biases = [
        bias_of(section, plan_ref, refresh_ref) for section in (me - 3 * sign, me + sign - 2, me + sign + 2)
    ]
    readers = [moved(block) for block in (far_ref, beside_behind_ref, beside_ahead_ref)]
    for head, (_, total, mixed) in absorbed(query_ref, readers, biases, (top_in, sum_in, acc_in)):
        done = (mixed / jnp.sum(total, axis=1, keepdims=True)).astype(jnp.bfloat16)
        out_ref[:, :, columns(head)] = done.reshape(out_ref.shape[0], out_ref.shape[1], HD)


SMEM_SPEC = pl.BlockSpec(memory_space=pltpu.SMEM)
VMEM_SPEC = pl.BlockSpec(memory_space=pltpu.VMEM)
STATE = (jax.ShapeDtypeStruct((LOCAL, PT, HD), jnp.float32),) * 3


def patches(count):
    return [pltpu.VMEM((2, count, PT, WIDE), jnp.bfloat16), pltpu.SemaphoreType.DMA((count,))]


def run(kernel, blocks, scalars, arrays, out_shape, scratch, cache=()):
    keys = blocks * PT
    return pl.pallas_call(
        kernel,
        out_shape=out_shape,
        in_specs=[SMEM_SPEC] * len(scalars) + [pl.BlockSpec(memory_space=pl.ANY)] * len(cache) + [VMEM_SPEC] * len(arrays),
        out_specs=jax.tree.map(lambda _: VMEM_SPEC, out_shape),
        scratch_shapes=scratch,
        compiler_params=pltpu.CompilerParams(vmem_limit_bytes=VMEM_BYTES),
        cost_estimate=pl.CostEstimate(
            flops=8 * LOCAL * PT * keys * HD, bytes_accessed=2 * keys * WIDE * 2, transcendentals=LOCAL * PT * keys
        ),
    )(*scalars, *cache, *arrays)


def stale_order(scalars, cache):
    return pl.pallas_call(
        order_kernel,
        out_shape=(
            jax.ShapeDtypeStruct((PATCHES + 1,), jnp.int32), jax.ShapeDtypeStruct((2, GROUP, PT, WIDE), cache.dtype)
        ),
        in_specs=[SMEM_SPEC] * 3 + [pl.BlockSpec(memory_space=pl.ANY)],
        out_specs=(SMEM_SPEC, VMEM_SPEC),
        scratch_shapes=[pltpu.SemaphoreType.DMA((GROUP,))],
        compiler_params=pltpu.CompilerParams(vmem_limit_bytes=VMEM_BYTES),
    )(*scalars, cache)


def move(value, target):
    count = lax.axis_size("pipe")
    return lax.ppermute(value, "pipe", [(source, target(source) % count) for source in range(count)])


def exchange(value):
    return lax.all_to_all(value, "uly", split_axis=0, concat_axis=0, tiled=True)


def shards(fresh_qkv, stale_cache, plan, refresh):
    rows = fresh_qkv.shape[0]
    devices = lax.axis_size("uly")
    me = lax.axis_index("pipe").astype(jnp.int32)
    scalars = (me.reshape(1), plan, refresh)
    outgoing = fresh_qkv.reshape(rows, 3, devices, WIDE).transpose(2, 1, 0, 3)
    heads = exchange(outgoing)
    cache = stale_cache[0].transpose(1, 0, 2)
    order, early = stale_order(scalars, cache)
    heads, cache, order, early = lax.optimization_barrier((heads, cache, order, early))
    own, query = heads[:, 1:3], heads[:, 0]
    twin = lambda s: s ^ 1
    behind = move(own, lambda s: s + 2)
    ahead = move(own, lambda s: s - 2)
    beside = move(own, twin)
    state = run(first_kernel, FIRST, (order,), (query, early), STATE, patches(FIRST - GROUP), (cache,))
    state, behind, ahead = lax.optimization_barrier((state, behind, ahead))
    beside_behind = move(behind, twin)
    beside_ahead = move(ahead, twin)
    far = move(jnp.where(me % 2 == 1, behind, ahead), lambda s: s + 1 if s % 2 else s - 1)
    state = run(
        second_kernel, 8, (*scalars, order), (query, *state, own, beside, behind, ahead), STATE,
        patches(PATCHES - 1 - FIRST), (cache,),
    )
    mixed = run(
        last_kernel, 3, scalars, (query, *state, far, beside_behind, beside_ahead),
        jax.ShapeDtypeStruct(query.shape, jnp.bfloat16), [],
    )
    back = exchange(mixed)
    return back.transpose(1, 0, 2).reshape(rows, devices * WIDE)


def solution(mesh):
    placed = (P(("pipe", "uly"), None, None), P("pipe", None, None, "uly"), P(), P("pipe", None))
    return jax.shard_map(
        shards, mesh=mesh, in_specs=placed, out_specs=P(("pipe", "uly"), None), check_vma=False
    )
```

```python
import math

import jax
import jax.numpy as jnp
from jax import lax
from jax.experimental import pallas as pl
from jax.experimental.pallas import tpu as pltpu
from jax.sharding import PartitionSpec as P

HD = 128
PT = 256
LOCAL = 3
WIDE = LOCAL * HD
PATCHES = 32
SLOTS = 6
SCALE = math.log2(math.e) / math.sqrt(HD)
GROUP = 6
FIRST = 24
VMEM_BYTES = 48 * 1024 * 1024


def columns(head):
    return slice(head * HD, (head + 1) * HD)


def absorb(head, scores, values, biases, top_ref, sum_ref, acc_ref):
    before = top_ref[head]
    top = before
    for score, bias in zip(scores, biases):
        widest = score[:, :HD]
        for start in range(HD, PT, HD):
            widest = jnp.maximum(widest, score[:, start:start + HD])
        widest = widest * SCALE
        top = jnp.maximum(top, widest if bias is None else widest + bias)
    top = jnp.broadcast_to(jnp.max(top, axis=1, keepdims=True), top.shape)
    fade = jnp.exp2(before - top)
    total = sum_ref[head] * fade
    mixed = acc_ref[head] * fade
    for score, value, bias in zip(scores, values, biases):
        level = top if bias is None else top - bias
        parts = []
        for start in range(0, PT, HD):
            probs = jnp.exp2(score[:, start:start + HD] * SCALE - level)
            total = total + probs
            parts.append(probs.astype(jnp.bfloat16))
        weights = jnp.concatenate(parts, axis=1)
        mixed = mixed + jnp.dot(weights, value, preferred_element_type=jnp.float32)
    acc_ref[head] = mixed
    sum_ref[head] = total
    top_ref[head] = top


def attend(query_ref, readers, biases, state):
    scores = []
    for head in range(LOCAL):
        query = query_ref[:, :, columns(head)].reshape(PT, HD)
        scores.append([
            lax.dot_general(query, read(0, head), (((1,), (1,)), ((), ())), preferred_element_type=jnp.float32)
            for read in readers
        ])
    for head in range(LOCAL):
        absorb(head, scores[head], [read(1, head) for read in readers], biases, *state)


def cached(held, place):
    return lambda part, head: held[part, place, :, columns(head)]


def moved(block_ref):
    return lambda part, head: block_ref[:, part, :, columns(head)].reshape(PT, HD)


def listing(patch, refresh_ref):
    found = refresh_ref[0, 0] == patch
    for slot in range(1, SLOTS):
        found = jnp.logical_or(found, refresh_ref[0, slot] == patch)
    return found


def bias_of(section, plan_ref, refresh_ref):
    patch = plan_ref[(section + PATCHES) % PATCHES]
    return jnp.where(listing(patch, refresh_ref), 0.0, -jnp.inf).astype(jnp.float32)


def fetch(patch, place, cache_ref, held, arrived):
    return pltpu.make_async_copy(
        cache_ref.at[:, pl.ds(pl.multiple_of(patch * PT, PT), PT), :], held.at[:, place], arrived.at[place]
    )


def attend_stale(first, width, query_ref, cache_ref, held, arrived, state):
    for place in range(width):
        fetch(0, first + place, cache_ref, held, arrived).wait()
    attend(query_ref, [cached(held, first + place) for place in range(width)], [None] * width, state)


def sign_of(me):
    return jnp.where(me % 2 == 0, 1, -1)


def order_kernel(me_ref, plan_ref, refresh_ref, cache_ref, order_ref, early, arrived):
    one = jnp.int32(1)
    fresh = jnp.left_shift(one, plan_ref[me_ref[0]])
    for slot in range(SLOTS):
        patch = refresh_ref[0, slot]
        fresh = fresh | jnp.where(patch >= 0, jnp.left_shift(one, jnp.maximum(patch, 0)), 0)
    count = jnp.int32(0)
    for patch in range(PATCHES):
        order_ref[count] = jnp.int32(patch)
        count = count + 1 - (jnp.right_shift(fresh, patch) & 1)
    order_ref[PATCHES] = count
    copies = [fetch(order_ref[place], place, cache_ref, early, arrived) for place in range(GROUP)]
    for copy in copies:
        copy.start()
    for copy in copies:
        copy.wait()


def first_kernel(order_ref, cache_ref, query_ref, early, top_ref, sum_ref, acc_ref, held, arrived):
    def begin(group):
        for place in range(GROUP):
            place = group * GROUP + place
            fetch(order_ref[GROUP + place], place, cache_ref, held, arrived).start()

    for group in range(FIRST // GROUP - 1):
        begin(group)
    state = (top_ref, sum_ref, acc_ref)
    for target, value in zip(state, (-jnp.inf, 0.0, 0.0)):
        target[...] = jnp.full(target.shape, value, jnp.float32)
    attend(query_ref, [cached(early, place) for place in range(GROUP)], [None] * GROUP, state)

    @pl.loop(0, FIRST // GROUP - 1)
    def _(group):
        attend_stale(group * GROUP, GROUP, query_ref, cache_ref, held, arrived, state)


def second_kernel(me_ref, plan_ref, refresh_ref, order_ref, cache_ref, query_ref, top_in, sum_in, acc_in, own_ref,
                  beside_ref, behind_ref, ahead_ref, top_ref, sum_ref, acc_ref, held, arrived):
    left = order_ref[PATCHES] - FIRST

    @pl.loop(0, left)
    def _(place):
        fetch(order_ref[FIRST + place], place, cache_ref, held, arrived).start()

    state = (top_ref, sum_ref, acc_ref)
    for source, target in zip((top_in, sum_in, acc_in), state):
        target[...] = source[...]
    me = me_ref[0]
    biases = [None] + [
        bias_of(section, plan_ref, refresh_ref) for section in (me + sign_of(me), me - 2, me + 2)
    ]
    readers = [moved(block) for block in (own_ref, beside_ref, behind_ref, ahead_ref)]
    attend(query_ref, readers, biases, state)

    @pl.when(left >= 4)
    def _():
        attend_stale(0, 4, query_ref, cache_ref, held, arrived, state)

    done = jnp.where(left >= 4, 4, 0)
    for width in range(1, 4):

        @pl.when(left - done == width)
        def _(width=width):
            attend_stale(done, width, query_ref, cache_ref, held, arrived, state)


def last_kernel(me_ref, plan_ref, refresh_ref, query_ref, top_in, sum_in, acc_in, far_ref, beside_behind_ref,
                beside_ahead_ref, out_ref, top_ref, sum_ref, acc_ref):
    state = (top_ref, sum_ref, acc_ref)
    for source, target in zip((top_in, sum_in, acc_in), state):
        target[...] = source[...]
    me = me_ref[0]
    sign = sign_of(me)
    biases = [
        bias_of(section, plan_ref, refresh_ref) for section in (me - 3 * sign, me + sign - 2, me + sign + 2)
    ]
    readers = [moved(block) for block in (far_ref, beside_behind_ref, beside_ahead_ref)]
    attend(query_ref, readers, biases, state)
    for head in range(LOCAL):
        total = jnp.sum(sum_ref[head], axis=1, keepdims=True)
        done = (acc_ref[head] / total).astype(jnp.bfloat16)
        out_ref[:, :, columns(head)] = done.reshape(out_ref.shape[0], out_ref.shape[1], HD)


SMEM_SPEC = pl.BlockSpec(memory_space=pltpu.SMEM)
VMEM_SPEC = pl.BlockSpec(memory_space=pltpu.VMEM)
STATE = (jax.ShapeDtypeStruct((LOCAL, PT, HD), jnp.float32),) * 3


def patches(count):
    return [pltpu.VMEM((2, count, PT, WIDE), jnp.bfloat16), pltpu.SemaphoreType.DMA((count,))]


def run(kernel, blocks, scalars, arrays, out_shape, scratch, cache=()):
    keys = blocks * PT
    return pl.pallas_call(
        kernel,
        out_shape=out_shape,
        in_specs=[SMEM_SPEC] * len(scalars) + [pl.BlockSpec(memory_space=pl.ANY)] * len(cache) + [VMEM_SPEC] * len(arrays),
        out_specs=jax.tree.map(lambda _: VMEM_SPEC, out_shape),
        scratch_shapes=scratch,
        compiler_params=pltpu.CompilerParams(vmem_limit_bytes=VMEM_BYTES),
        cost_estimate=pl.CostEstimate(
            flops=8 * LOCAL * PT * keys * HD, bytes_accessed=2 * keys * WIDE * 2, transcendentals=LOCAL * PT * keys
        ),
    )(*scalars, *cache, *arrays)


def stale_order(scalars, cache):
    return pl.pallas_call(
        order_kernel,
        out_shape=(
            jax.ShapeDtypeStruct((PATCHES + 1,), jnp.int32), jax.ShapeDtypeStruct((2, GROUP, PT, WIDE), cache.dtype)
        ),
        in_specs=[SMEM_SPEC] * 3 + [pl.BlockSpec(memory_space=pl.ANY)],
        out_specs=(SMEM_SPEC, VMEM_SPEC),
        scratch_shapes=[pltpu.SemaphoreType.DMA((GROUP,))],
        compiler_params=pltpu.CompilerParams(vmem_limit_bytes=VMEM_BYTES),
    )(*scalars, cache)


def move(value, target):
    count = lax.axis_size("pipe")
    return lax.ppermute(value, "pipe", [(source, target(source) % count) for source in range(count)])


def exchange(value):
    return lax.all_to_all(value, "uly", split_axis=0, concat_axis=0, tiled=True)


def shards(fresh_qkv, stale_cache, plan, refresh):
    rows = fresh_qkv.shape[0]
    devices = lax.axis_size("uly")
    me = lax.axis_index("pipe").astype(jnp.int32)
    scalars = (me.reshape(1), plan, refresh)
    outgoing = fresh_qkv.reshape(rows, 3, devices, WIDE).transpose(2, 1, 0, 3)
    heads = exchange(outgoing)
    cache = stale_cache[0].transpose(1, 0, 2)
    order, early = stale_order(scalars, cache)
    heads, cache, order, early = lax.optimization_barrier((heads, cache, order, early))
    own, query = heads[:, 1:3], heads[:, 0]
    twin = lambda s: s ^ 1
    behind = move(own, lambda s: s + 2)
    ahead = move(own, lambda s: s - 2)
    beside = move(own, twin)
    state = run(first_kernel, FIRST, (order,), (query, early), STATE, patches(FIRST - GROUP), (cache,))
    state, behind, ahead = lax.optimization_barrier((state, behind, ahead))
    beside_behind = move(behind, twin)
    beside_ahead = move(ahead, twin)
    far = move(jnp.where(me % 2 == 1, behind, ahead), lambda s: s + 1 if s % 2 else s - 1)
    state = run(
        second_kernel, 8, (*scalars, order), (query, *state, own, beside, behind, ahead), STATE,
        patches(PATCHES - 1 - FIRST), (cache,),
    )
    held = pltpu.VMEM((LOCAL, PT, HD), jnp.float32)
    mixed = run(
        last_kernel, 3, scalars, (query, *state, far, beside_behind, beside_ahead),
        jax.ShapeDtypeStruct(query.shape, jnp.bfloat16), [held] * 3,
    )
    back = exchange(mixed)
    return back.transpose(1, 0, 2).reshape(rows, devices * WIDE)


def solution(mesh):
    placed = (P(("pipe", "uly"), None, None), P("pipe", None, None, "uly"), P(), P("pipe", None))
    return jax.shard_map(
        shards, mesh=mesh, in_specs=placed, out_specs=P(("pipe", "uly"), None), check_vma=False
    )
```
